512 devices in a mesh: vocab: 32 (over y, x, core), rows: 16 (over z).
Axes of the slice: x: 4, y: 4, z: 16, core: 2. Of those that a mesh axis runs over, the one named last changes fastest.
Arguments:
- h_student: bfloat16 [384, 2560], P('rows'), may hold values from -6 to 6, as said below
- h_teacher: bfloat16 [384, 5120], P('rows'), may hold values from -6 to 6, as said below
- w_student: bfloat16 [98304, 2560], P(('vocab', 'rows')), may hold values from -1 to 1, as said below
- w_teacher: bfloat16 [98304, 5120], P(('vocab', 'rows')), may hold values from -1 to 1, as said below
Outputs:
- losses: float32 [2, 384], P(None, 'rows')
- d_hidden: float32 [384, 2560], P('rows', 'vocab')
- d_weight: bfloat16 [98304, 2560], P(('vocab', 'rows'))
The draws below stay inside these ranges and needn't reach their ends.
Inputs may be any that keep to these rules, and one draw needn't show every extreme that they name: `h_student`: real-valued hidden states. `h_teacher`: real-valued hidden states. `w_student`: real-valued embedding rows. `w_teacher`: real-valued embedding rows.
All inputs are finite; a program needn't handle non-finite values.
Results may differ from the reference program's by a relative error of at most 0.03.
Values may be sent and summed in bfloat16 or wider, within the bound.
No kernel may reach another device: no remote copies, remote signals or barrier semaphores. Data moves between devices by JAX's collectives and lax.ppermute only.
A program may use at most 64 MiB of HBM per device.

```python
import math
import jax
import jax.numpy as jnp

DS = 2560
DT = 5120
TOKENS = 384
VOCAB = 98304


def draw_h_student(key, part):
    key = jax.random.fold_in(key, 3)
    return jnp.clip(jax.random.normal(key, (TOKENS, DS), jnp.float32), -6.0, 6.0).astype(jnp.bfloat16)


def draw_h_teacher(key, part):
    key = jax.random.fold_in(key, 4)
    return jnp.clip(jax.random.normal(key, (TOKENS, DT), jnp.float32), -6.0, 6.0).astype(jnp.bfloat16)


def draw_w_student(key, part):
    key = jax.random.fold_in(key, 5)
    raw = jnp.clip(jax.random.normal(key, (VOCAB, DS), jnp.float32), -6.0, 6.0)
    position = jnp.arange(VOCAB, dtype=jnp.float32)[:, None] / VOCAB
    return (raw * (0.5 + 0.24 * position) * (3.0 / math.sqrt(DS))).astype(jnp.bfloat16)


def draw_w_teacher(key, part):
    key = jax.random.fold_in(key, 6)
    raw = jnp.clip(jax.random.normal(key, (VOCAB, DT), jnp.float32), -6.0, 6.0)
    position = jnp.arange(VOCAB, dtype=jnp.float32)[:, None] / VOCAB
    return (raw * (0.5 + 0.24 * position) * (3.0 / math.sqrt(DT))).astype(jnp.bfloat16)


def setup_inputs(seed: int = 0) -> dict:
    seeds = jax.random.split(jax.random.key(seed), 5)
    h_student = draw_h_student(jax.random.fold_in(seeds[4], 71), 0)
    h_teacher = draw_h_teacher(jax.random.fold_in(seeds[4], 71), 0)
    w_student = draw_w_student(jax.random.fold_in(seeds[4], 71), 0)
    w_teacher = draw_w_teacher(jax.random.fold_in(seeds[4], 71), 0)
    return dict(h_student=h_student, h_teacher=h_teacher, w_student=w_student, w_teacher=w_teacher)


skew_mix = 0.1


def reference(h_student, h_teacher, w_student, w_teacher):
    student_logits = jnp.dot(h_student, w_student.T, preferred_element_type=jnp.float32)
    teacher_logits = jnp.dot(h_teacher, w_teacher.T, preferred_element_type=jnp.float32)
    student_top = jnp.max(student_logits, axis=1, keepdims=True)
    teacher_top = jnp.max(teacher_logits, axis=1, keepdims=True)
    student_total = jnp.sum(jnp.exp(student_logits - student_top), axis=1, keepdims=True)
    teacher_total = jnp.sum(jnp.exp(teacher_logits - teacher_top), axis=1, keepdims=True)
    log_q = student_logits - student_top - jnp.log(student_total)
    log_p = teacher_logits - teacher_top - jnp.log(teacher_total)
    prob_q = jnp.exp(log_q)
    prob_p = jnp.exp(log_p)
    log_mix_fwd = jnp.logaddexp(jnp.log(skew_mix) + log_p, jnp.log(1.0 - skew_mix) + log_q)
    log_mix_rev = jnp.logaddexp(jnp.log(1.0 - skew_mix) + log_p, jnp.log(skew_mix) + log_q)
    forward_kl = jnp.sum(prob_p * (log_p - log_mix_fwd), axis=1)
    reverse_kl = jnp.sum(prob_q * (log_q - log_mix_rev), axis=1)
    grad_q = (-(1.0 - skew_mix) * jnp.exp(log_p - log_mix_fwd) + log_q - log_mix_rev
              - skew_mix * jnp.exp(log_q - log_mix_rev))
    inner = jnp.sum(prob_q * grad_q, axis=1, keepdims=True)
    logit_grad = (prob_q * (grad_q - inner)).astype(jnp.bfloat16)
    d_hidden = jnp.dot(logit_grad, w_student, preferred_element_type=jnp.float32)
    d_weight = jnp.dot(logit_grad.T, h_student, preferred_element_type=jnp.float32).astype(jnp.bfloat16)
    return jnp.stack([forward_kl, reverse_kl]), d_hidden, d_weight
```

```python
import jax
import jax.numpy as jnp
from jax import lax
from jax.experimental import pallas as pl
from jax.experimental.pallas import tpu as pltpu
from jax.sharding import Mesh, PartitionSpec as P

skew_mix = 0.1
f32, bf16 = jnp.float32, jnp.bfloat16
PLANE = ("y", "x")
VOCAB = ("y", "x", "core")
EVERY = ("y", "x", "core", "rows")
NT = (((1,), (1,)), ((), ()))
NN = (((1,), (0,)), ((), ()))
MIB = 1024 * 1024


def params(mib=24, **kw):
    return pltpu.CompilerParams(vmem_limit_bytes=mib * MIB, **kw)


def cost(flops, nbytes, trans=0):
    return pl.CostEstimate(flops=flops, bytes_accessed=nbytes, transcendentals=trans)


def sds(shape, dtype):
    return jax.ShapeDtypeStruct(shape, dtype)


def lse(a, axis):
    top = jnp.max(a, axis=axis, keepdims=True)
    return top + jnp.log(jnp.sum(jnp.exp(a - top), axis=axis, keepdims=True))


def five(h_ref, w_ref):
    acc = None
    for k in range(5):
        part = lax.dot_general(
            w_ref[:, 256 * k : 256 * (k + 1)], h_ref[k], NT, preferred_element_type=f32
        )
        acc = part if acc is None else acc + part
    return acc


def half_kernel(core_ref, h_ref, ws_ref, wt_ref, out_ref):
    i = pl.program_id(0)

    @pl.when(i == 0)
    def _():
        out_ref[0] = five(h_ref, ws_ref)

    @pl.when(i == 1)
    def _():
        out_ref[1] = five(h_ref, wt_ref)

    @pl.when(i == 2)
    def _():
        out_ref[1] += five(h_ref, wt_ref)


def rest_kernel(core_ref, h_ref, ws_ref, wt_ref, part_ref, out_ref, lse_ref):
    i = pl.program_id(0)

    @pl.when(i == 0)
    def _():
        out_ref[0] = part_ref[0] + five(h_ref, ws_ref)

    @pl.when(i == 1)
    def _():
        out_ref[1] = part_ref[1] + five(h_ref, wt_ref)

    @pl.when(i == 2)
    def _():
        out_ref[1] += five(h_ref, wt_ref)
        both = jnp.concatenate([lse(out_ref[0], 0), lse(out_ref[1], 0)], axis=0)
        lse_ref[...] = jnp.broadcast_to(both[None], lse_ref.shape)


def logits_call(kernel, core, h, w_s, w_t, flip, part=None):
    ent, tok = w_s.shape[0], h.shape[1]
    in_specs = [
        pl.BlockSpec((5, tok, 256), lambda i, c: (i, 0, 0)),
        pl.BlockSpec((ent, 1280), lambda i, c: (0, c[0] ^ flip)),
        pl.BlockSpec((ent, 1280), lambda i, c: (0, 2 * (c[0] ^ flip) + jnp.maximum(i - 1, 0))),
    ]
    whole = pl.BlockSpec((2, ent, tok), lambda i, c: (0, 0, 0))
    out_shape, out_specs, args = [sds((2, ent, tok), f32)], [whole], [core, h, w_s, w_t]
    if part is not None:
        in_specs.append(whole)
        args.append(part)
        out_shape.append(sds((32, 2, tok), f32))
        out_specs.append(pl.BlockSpec((32, 2, tok), lambda i, c: (0, 0, 0)))
    return pl.pallas_call(
        kernel,
        grid_spec=pltpu.PrefetchScalarGridSpec(
            num_scalar_prefetch=1, grid=(3,), in_specs=in_specs, out_specs=out_specs
        ),
        out_shape=out_shape,
        compiler_params=params(),
        cost_estimate=cost(2 * ent * tok * 3840, 6_000_000, 150_000 if part is not None else 0),
    )(*args)


def merge_lse_kernel(a_ref, out_ref):
    out_ref[...] = jnp.broadcast_to(lse(a_ref[...], 0), out_ref.shape)


def minus_logaddexp(a, d):
    return -(jnp.maximum(a, d) + jnp.log1p(jnp.exp(-jnp.abs(a - d))))


def entries_kernel(norm_ref, logit_ref, qg_ref, sum_ref):
    norm = lse(norm_ref[...], 0)[0]
    log_q = logit_ref[0] - norm[0:1]
    log_p = logit_ref[1] - norm[1:2]
    d = log_p - log_q
    low, high = jnp.log(f32(skew_mix)), jnp.log(f32(1.0 - skew_mix))
    fwd = minus_logaddexp(low, high - d)
    rev = minus_logaddexp(high + d, low)
    q = jnp.exp(log_q)
    grad = -(1.0 - skew_mix) * jnp.exp(fwd) + rev - skew_mix * jnp.exp(rev)
    qg_ref[0] = q
    qg_ref[1] = grad
    sums = [
        jnp.sum(q * grad, axis=0, keepdims=True),
        jnp.sum(jnp.exp(log_p) * fwd, axis=0, keepdims=True),
        jnp.sum(q * rev, axis=0, keepdims=True),
    ]
    sum_ref[...] = jnp.broadcast_to(jnp.concatenate(sums, axis=0)[None], sum_ref.shape)


def merge_sum_kernel(a_ref, inner_ref, loss_ref):
    total = jnp.sum(a_ref[...], axis=0)
    inner_ref[...] = jnp.broadcast_to(total[None, 0:1], inner_ref.shape)
    loss_ref[...] = total[1:3]


def grad_kernel(inner_ref, own_ref, peer_ref, wt_own_ref, wt_peer_ref, lg_ref, dh_ref):
    inner = jnp.sum(inner_ref[...], axis=0)
    own = (own_ref[0] * (own_ref[1] - inner)).astype(bf16)
    peer = (peer_ref[0] * (peer_ref[1] - inner)).astype(bf16)
    lg_ref[...] = own
    for k in range(5):
        at = slice(256 * k, 256 * (k + 1))
        dh_ref[at, :] = (
            lax.dot_general(wt_own_ref[at, :], own, NN, preferred_element_type=f32)
            + lax.dot_general(wt_peer_ref[at, :], peer, NN, preferred_element_type=f32)
        ).astype(bf16)


def weight_kernel(core_ref, lg_ref, own_ref, peer_ref, out_ref):
    def fill(h_ref):
        for k in range(5):
            out_ref[:, 256 * k : 256 * (k + 1)] = lax.dot_general(
                lg_ref[...], h_ref[k], NN, preferred_element_type=f32
            ).astype(bf16)

    @pl.when(pl.program_id(0) == 0)
    def _():
        fill(own_ref)

    @pl.when(pl.program_id(0) == 1)
    def _():
        fill(peer_ref)


def plane_sum_kernel(a_ref, loss_ref, out_ref):
    total = jnp.sum(a_ref[...].astype(f32), axis=0)
    loss = loss_ref[...]
    high = loss.astype(bf16).astype(f32)
    mid = (loss - high).astype(bf16).astype(f32)
    rest = loss - high - mid
    pad = jnp.zeros((128 - total.shape[0] - 6, total.shape[1]), f32)
    out_ref[...] = jnp.concatenate([total, high, mid, rest, pad], axis=0).T.astype(bf16)


def rows_sum_kernel(a_ref, dh_ref, loss_ref):
    total = jnp.sum(a_ref[...].astype(f32), axis=0)
    cols, tok = dh_ref.shape[1], dh_ref.shape[0]
    dh_ref[...] = total[:, :cols]
    square = jnp.concatenate([total, jnp.zeros((128 - tok, 128), f32)], axis=0).T
    parts = square[cols : cols + 8]
    loss_ref[...] = (parts[0:2] + parts[2:4] + parts[4:6])[:, :tok]


def call(kernel, out_shape, *args, mib=24, flops=0, nbytes=1_000_000, trans=0):
    return pl.pallas_call(
        kernel,
        out_shape=out_shape,
        compiler_params=params(mib),
        cost_estimate=cost(flops, nbytes, trans),
    )(*args)


def copies(x, n):
    return jnp.broadcast_to(x[None], (n,) + x.shape)


def exchange(x, axes):
    return lax.all_to_all(x, axes, 0, 0)


def local(h_s, h_t, w_s, w_t):
    core = lax.axis_index("core")
    at = lax.axis_index(PLANE)
    core_arr = jnp.reshape(core, (1,)).astype(jnp.int32)
    swap = [(0, 1), (1, 0)]

    part_s = lax.dynamic_slice(h_s, (0, 1280 * core + 256 * jnp.minimum(at, 4)), (24, 256))
    part_t = lax.dynamic_slice(h_t, (0, 2560 * core + 256 * jnp.clip(at - 5, 0, 9)), (24, 256))
    piece = jnp.where(at < 5, part_s, part_t)
    tokens = exchange(copies(piece, 16), "rows").reshape(384, 256)
    own_h = exchange(copies(tokens, 16), PLANE)
    peer_h = lax.ppermute(own_h, "core", swap)

    by_core = w_s.reshape(192, 16, 2, 80).transpose(2, 1, 3, 0).reshape(2, 1280, 192)
    wt_own = lax.dynamic_index_in_dim(by_core, core, 0, keepdims=False)
    wt_peer = lax.ppermute(
        lax.dynamic_index_in_dim(by_core, 1 - core, 0, keepdims=False), "core", swap
    )

    (part,) = logits_call(half_kernel, core_arr, own_h, w_s, w_t, 0)
    logits, norm = logits_call(rest_kernel, core_arr, peer_h, w_s, w_t, 1, part)

    norm = call(merge_lse_kernel, sds((16, 2, 384), f32), exchange(norm, VOCAB))
    norm = exchange(norm, "rows")
    qg, sums = call(
        entries_kernel, [sds((2, 192, 384), f32), sds((32, 3, 384), f32)], norm, logits,
        nbytes=1_200_000, trans=600_000,
    )
    peer_qg = lax.ppermute(qg, "core", swap)
    inner, loss = call(
        merge_sum_kernel, [sds((16, 1, 384), f32), sds((2, 384), f32)], exchange(sums, VOCAB)
    )
    inner = exchange(inner, "rows")
    lg, dh = call(
        grad_kernel, [sds((192, 384), bf16), sds((1280, 384), bf16)],
        inner, qg, peer_qg, wt_own, wt_peer, flops=2 * 384 * 384 * 1280, nbytes=3_000_000,
    )
    d_weight = pl.pallas_call(
        weight_kernel,
        grid_spec=pltpu.PrefetchScalarGridSpec(
            num_scalar_prefetch=1,
            grid=(2,),
            in_specs=[
                pl.BlockSpec((192, 384), lambda i, c: (0, 0)),
                pl.BlockSpec((5, 384, 256), lambda i, c: (0, 0, 0)),
                pl.BlockSpec((5, 384, 256), lambda i, c: (0, 0, 0)),
            ],
            out_specs=pl.BlockSpec((192, 1280), lambda i, c: (0, c[0] ^ i)),
        ),
        out_shape=sds((192, 2560), bf16),
        compiler_params=params(),
        cost_estimate=cost(2 * 192 * 384 * 2560, 3_000_000),
    )(core_arr, lg, own_h, peer_h)

    dh = exchange(dh.reshape(16, 80, 384), PLANE)
    dh = call(plane_sum_kernel, sds((384, 128), bf16), dh, loss)
    dh = exchange(dh.reshape(16, 24, 128), "rows")
    d_hidden, losses = call(rows_sum_kernel, [sds((24, 80), f32), sds((2, 24), f32)], dh)
    return losses, d_hidden, d_weight


def solution(mesh):
    grid = Mesh(mesh.devices.reshape(4, 4, 2, 16), EVERY)
    return jax.shard_map(
        local,
        mesh=grid,
        in_specs=(P("rows", None), P("rows", None), P(EVERY, None), P(EVERY, None)),
        out_specs=(P(None, "rows"), P("rows", VOCAB), P(EVERY, None)),
        check_vma=False,
    )
```
